512 devices in a mesh: leaf: 16 (over z_hi, x, core), node: 32 (over y, z_lo).
Axes of the slice: x: 4, y: 4, z: 16 (z_hi: 2, z_lo: 8; z = z_hi * 8 + z_lo), core: 2. Of those that a mesh axis runs over, the one named last changes fastest.
Arguments:
- queries: bfloat16 [65536, 4096], P(('leaf', 'node')), parts along dimension 0, may hold values from -60 to 60
- key_states: bfloat16 [65536, 512], P(('leaf', 'node')), parts along dimension 0, may hold values from -4 to 4
- state_values: bfloat16 [65536, 512], P(('leaf', 'node')), parts along dimension 0, may hold values from -4 to 4
- out_grad: bfloat16 [65536, 4096], P(('leaf', 'node')), parts along dimension 0, may hold values from -4 to 4
- block_depth: int32 [512], P('leaf'), parts along dimension 0, may hold values from 0 to 3, as said below
Outputs:
- attended: bfloat16 [65536, 4096], P(('leaf', 'node')), parts along dimension 0
- query_grad: bfloat16 [65536, 4096], P(('leaf', 'node')), parts along dimension 0
- key_grad: bfloat16 [65536, 512], P(('leaf', 'node')), parts along dimension 0
- value_grad: bfloat16 [65536, 512], P(('leaf', 'node')), parts along dimension 0
The draws below stay inside these ranges and needn't reach their ends.
There are 16 independent parts, one for each index of `leaf`. The reference program is written for one: setup_inputs(seed, part) draws one part's arguments, and reference() takes and returns one part's arrays. A program takes and returns all parts, laid end to end along the dimension named above; each array names one. Nothing has to cross between parts.
Inputs may be any that keep to these rules, and one draw needn't show every extreme that they name: block_depth[0] = 0; every later block has depth 1 to one more than the block before it; some block has depth 4 - 1.
All inputs are finite; a program needn't handle non-finite values.
Results may differ from the reference program's by a relative error of at most 0.035.
Values may be sent and summed in bfloat16 or wider, within the bound.
No kernel may reach another device: no remote copies, remote signals or barrier semaphores. Data moves between devices by JAX's collectives and lax.ppermute only.
A program may use at most 128 MiB of HBM per device.

```python
import jax
import jax.numpy as jnp
from jax import lax

TOK_DEV = 128
QUERY_HEADS = 32
KEY_VALUE_HEADS = 4
HEAD_SIZE = 128
DEPTH = 4
NBLK = 32
TREE_TOKENS = 4096


def draw_queries(key, part):
    self_key = jax.random.fold_in(key, 3)
    result_rows = jnp.clip(jax.random.normal(self_key, (TREE_TOKENS, QUERY_HEADS, HEAD_SIZE), jnp.float32), -4.0, 4.0)
    return result_rows.reshape(TREE_TOKENS, QUERY_HEADS * HEAD_SIZE).astype(jnp.bfloat16)


def draw_key_states(key, part):
    self_key = jax.random.fold_in(key, 5)
    ground_field = jnp.clip(jax.random.normal(self_key, (TREE_TOKENS, KEY_VALUE_HEADS, HEAD_SIZE), jnp.float32), -4.0, 4.0)
    return ground_field.reshape(TREE_TOKENS, KEY_VALUE_HEADS * HEAD_SIZE).astype(jnp.bfloat16)


def draw_block_depth(key, part):
    key = jax.random.fold_in(key, 7)
    go_deeper = jax.random.randint(jax.random.fold_in(key, 1), (NBLK,), 0, 2).astype(jnp.int32)
    chain_start = jax.random.randint(jax.random.fold_in(key, 2), (), 1, NBLK - DEPTH + 2).astype(jnp.int32)

    def advance(previous, inputs):
        block_id, deeper = inputs
        chosen_depth = jnp.where(deeper == 1, jnp.minimum(previous + 1, DEPTH - 1), 1)
        in_chain = (block_id >= chain_start) & (block_id < chain_start + DEPTH - 1)
        chosen_depth = jnp.where(in_chain, block_id - chain_start + 1, chosen_depth)
        chosen_depth = jnp.where(block_id == 0, 0, chosen_depth).astype(jnp.int32)
        return (chosen_depth, chosen_depth)
    final_depth, depths = lax.scan(advance, jnp.int32(0), (jnp.arange(NBLK, dtype=jnp.int32), go_deeper))
    return depths.astype(jnp.int32)


def level_of(rng, extent, split, smallest, largest):
    factor_of = 1.0
    for axis_at, parts in split:
        steps = jax.random.uniform(jax.random.fold_in(jax.random.fold_in(rng, 6), axis_at), (parts,), jnp.float32, smallest / len(split), largest / len(split))
        factor_of = factor_of * jnp.repeat(jnp.exp(steps), extent[axis_at] // parts).reshape((-1,) + (1,) * (len(extent) - 1 - axis_at))
    return factor_of


def bell_draw(key, shape, scale, limit, shards=(), kind=jnp.bfloat16):
    factor_of = level_of(key, shape, shards, -0.22, 0.18) if shards else 1.0
    array = jax.random.normal(key, shape, jnp.float32) * scale * factor_of
    return jnp.minimum(jnp.maximum(array, -limit), limit).astype(kind)


def setup_inputs(seed: int = 0, part: int = 0) -> dict:
    streams_of = jax.random.split(jax.random.key(seed), 6)
    part_splits = jax.random.split(jax.random.fold_in(streams_of[5], part), 6)
    queries = draw_queries(jax.random.fold_in(jax.random.fold_in(streams_of[5], part), 71), part)
    key_states = draw_key_states(jax.random.fold_in(jax.random.fold_in(streams_of[5], part), 71), part)
    state_values = bell_draw(part_splits[2], (TREE_TOKENS, KEY_VALUE_HEADS * HEAD_SIZE), 1.0, 4.0, ((0, 32),))
    out_grad = bell_draw(part_splits[3], (TREE_TOKENS, QUERY_HEADS * HEAD_SIZE), 1.0, 4.0, ((0, 32),))
    block_depth = draw_block_depth(jax.random.fold_in(jax.random.fold_in(streams_of[5], part), 71), part)
    return dict(queries=queries, key_states=key_states, state_values=state_values, out_grad=out_grad, block_depth=block_depth)


def ancestor_table(block_depth):
    block_count = block_depth.shape[0]
    block_ids = jnp.arange(block_count, dtype=jnp.int32)
    depth_levels = jnp.arange(DEPTH, dtype=jnp.int32)
    found_at = (block_depth[None, :, None] == depth_levels[None, None, :]) & (block_ids[None, :, None] <= block_ids[:, None, None])
    latest = jnp.max(jnp.where(found_at, block_ids[None, :, None], -1), axis=1)
    slot_valid = depth_levels[None, :] <= block_depth[:, None]
    return jnp.where(slot_valid, latest, 0).astype(jnp.int32), slot_valid


def allowed_mask(own_depth, slot_valid, count_of_rows):
    depth_levels = jnp.arange(DEPTH, dtype=jnp.int32)
    positions = jnp.arange(count_of_rows, dtype=jnp.int32)
    causal = positions[None, :] <= positions[:, None]
    earlier = (depth_levels < own_depth)[None, :, None]
    same_block = (depth_levels == own_depth)[None, :, None] & causal[:, None, :]
    allowed = slot_valid[None, :, None] & (earlier | same_block)
    return allowed.reshape(count_of_rows, DEPTH * count_of_rows)


def block_attention(block_queries, block_keys, block_values, gradient_block, allowed):
    count_of_rows = block_queries.shape[0]
    group_members = QUERY_HEADS // KEY_VALUE_HEADS
    score_scale = HEAD_SIZE ** -0.5
    heads_of_query = block_queries.astype(jnp.float32).reshape(count_of_rows, KEY_VALUE_HEADS, group_members, HEAD_SIZE)
    heads_of_key = block_keys.astype(jnp.float32).reshape(-1, KEY_VALUE_HEADS, HEAD_SIZE)
    heads_of_value = block_values.astype(jnp.float32).reshape(-1, KEY_VALUE_HEADS, HEAD_SIZE)
    gradient_heads = gradient_block.astype(jnp.float32).reshape(count_of_rows, KEY_VALUE_HEADS, group_members, HEAD_SIZE)
    scores = jnp.einsum("tgjd,ugd->gjtu", heads_of_query, heads_of_key) * score_scale
    scores = jnp.where(allowed[None, None], scores, -jnp.inf)
    row_max = jnp.max(scores, axis=-1, keepdims=True)
    weights = jnp.exp(scores - row_max)
    softmax_probs = weights / jnp.sum(weights, axis=-1, keepdims=True)
    probs_low = lax.optimization_barrier(softmax_probs.astype(jnp.bfloat16)).astype(jnp.float32)
    attended = jnp.einsum("gjtu,ugd->tgjd", probs_low, heads_of_value).astype(jnp.bfloat16)
    attended_wide = lax.optimization_barrier(attended).astype(jnp.float32)
    row_delta = jnp.einsum("tgjd,tgjd->gjt", gradient_heads, attended_wide)
    dprobs = jnp.einsum("tgjd,ugd->gjtu", gradient_heads, heads_of_value)
    dscores = softmax_probs * (dprobs - row_delta[..., None])
    dscores_low = lax.optimization_barrier(dscores.astype(jnp.bfloat16)).astype(jnp.float32)
    query_grad = (jnp.einsum("gjtu,ugd->tgjd", dscores_low, heads_of_key) * score_scale).astype(jnp.bfloat16)
    key_portion = jnp.einsum("gjtu,tgjd->ugd", dscores_low, heads_of_query) * score_scale
    value_portion = jnp.einsum("gjtu,tgjd->ugd", probs_low, gradient_heads)
    return (attended.reshape(count_of_rows, QUERY_HEADS * HEAD_SIZE), query_grad.reshape(count_of_rows, QUERY_HEADS * HEAD_SIZE),
            key_portion.reshape(-1, KEY_VALUE_HEADS * HEAD_SIZE), value_portion.reshape(-1, KEY_VALUE_HEADS * HEAD_SIZE))


def reference(queries, key_states, state_values, out_grad, block_depth):
    block_count = block_depth.shape[0]
    feat_width = key_states.shape[1]
    anc_table, slot_valid = ancestor_table(block_depth)
    key_blocks = key_states.reshape(block_count, TOK_DEV, feat_width)
    value_blocks = state_values.reshape(block_count, TOK_DEV, feat_width)

    def one_block(carry_in, block_index):
        key_acc, value_acc = carry_in
        path_slots = anc_table[block_index]
        block_queries = lax.dynamic_slice_in_dim(queries, block_index * TOK_DEV, TOK_DEV, 0)
        gradient_block = lax.dynamic_slice_in_dim(out_grad, block_index * TOK_DEV, TOK_DEV, 0)
        key_path = key_blocks[path_slots].reshape(DEPTH * TOK_DEV, feat_width)
        value_path = value_blocks[path_slots].reshape(DEPTH * TOK_DEV, feat_width)
        allowed = allowed_mask(block_depth[block_index], slot_valid[block_index], TOK_DEV)
        attended, query_grad, key_portion, value_portion = block_attention(block_queries, key_path, value_path, gradient_block, allowed)
        key_acc = key_acc.at[path_slots].add(key_portion.reshape(DEPTH, TOK_DEV, feat_width))
        value_acc = value_acc.at[path_slots].add(value_portion.reshape(DEPTH, TOK_DEV, feat_width))
        return (key_acc, value_acc), (attended, query_grad)

    zeros_acc = jnp.zeros((block_count, TOK_DEV, feat_width), jnp.float32)
    (key_acc, value_acc), (attended, query_grad) = lax.scan(
        one_block, (zeros_acc, zeros_acc), jnp.arange(block_count, dtype=jnp.int32))
    total_rows = block_count * TOK_DEV
    return (attended.reshape(total_rows, QUERY_HEADS * HEAD_SIZE), query_grad.reshape(total_rows, QUERY_HEADS * HEAD_SIZE),
            key_acc.reshape(total_rows, feat_width).astype(jnp.bfloat16),
            value_acc.reshape(total_rows, feat_width).astype(jnp.bfloat16))
```

```python
import jax
import jax.numpy as jnp
from jax import lax
from jax.experimental import pallas as pl
from jax.experimental.pallas import tpu as pltpu
from jax.sharding import PartitionSpec as P

HEAD = 128
TOK = 128
KV_HEADS = 4
GROUP = 8
BLOCKS = 32
ROWS = 4
COLS = 8
UPPER = 3
SLICE = 32
SCALE = HEAD ** -0.5
LOG2E = 1.4426950408889634
NEG = -1e30
F32 = jnp.float32
BF16 = jnp.bfloat16
Z_GROUPS = [[y * COLS + z for z in range(COLS)] for y in range(ROWS)]
Y_GROUPS = [[y * COLS + z for y in range(ROWS)] for z in range(COLS)]


def last_at(depth_ref, start, stop, level, default):
    def step(j, found):
        return jnp.where(depth_ref[j] == level, j, found)

    return lax.fori_loop(start, stop, step, default)


def pick_kernel(depth_ref, node_ref, row_ref, out_ref, sems):
    start = (node_ref[0] // COLS) * COLS
    copies = []
    for level in range(UPPER):
        if level == 0:
            at = 0
        else:
            at = last_at(depth_ref, start, start + COLS, level, start) - start
        copies.append(pltpu.make_async_copy(row_ref.at[at], out_ref.at[level], sems.at[level]))
    for copy in copies:
        copy.start()
    for copy in copies:
        copy.wait()


def pick(depth, node, row):
    return pl.pallas_call(
        pick_kernel,
        out_shape=jax.ShapeDtypeStruct((UPPER,) + row.shape[1:], row.dtype),
        in_specs=[
            pl.BlockSpec(memory_space=pltpu.SMEM),
            pl.BlockSpec(memory_space=pltpu.SMEM),
            pl.BlockSpec(memory_space=pl.ANY),
        ],
        out_specs=pl.BlockSpec(memory_space=pl.ANY),
        scratch_shapes=[pltpu.SemaphoreType.DMA((UPPER,))],
        name="pick",
    )(depth, node, row)


def dot(a, b):
    return jnp.dot(a, b, preferred_element_type=F32)


PAIR = 2


def main_kernel(
    depth_ref, node_ref, q_ref, do_ref, own_ref, row_ref, col_ref,
    att_ref, dq_ref, up_ref, mine_ref,
    kv, sems,
):
    head = pl.program_id(0)
    node = node_ref[0]
    own_depth = depth_ref[node]

    @pl.when(head == 0)
    def _():
        y = node // COLS
        own_copy = pltpu.make_async_copy(own_ref, kv.at[UPPER], sems.at[UPPER])
        own_copy.start()
        for level in range(UPPER):
            if level == 0:
                at = 0
            else:
                at = last_at(depth_ref, 0, node + 1, level, 0)
            at_row = at // COLS

            @pl.when(at_row == y)
            def _():
                pltpu.make_async_copy(row_ref.at[at - at_row * COLS], kv.at[level], sems.at[level]).start()

            @pl.when(at_row != y)
            def _():
                pltpu.make_async_copy(col_ref.at[at_row, level], kv.at[level], sems.at[level]).start()

        for level in range(UPPER):
            pltpu.make_async_copy(row_ref.at[0], kv.at[level], sems.at[level]).wait()
        own_copy.wait()

    kcols = pl.ds(pl.multiple_of(head * HEAD, HEAD), HEAD)
    vcols = pl.ds(pl.multiple_of((KV_HEADS + head) * HEAD, HEAD), HEAD)
    keys = kv[:, :, kcols].reshape((UPPER + 1) * TOK, HEAD)
    values = kv[:, :, vcols].reshape((UPPER + 1) * TOK, HEAD)
    keys_t = keys.T
    values_t = values.T
    width = PAIR * TOK
    u = lax.broadcasted_iota(jnp.int32, (TOK, width), 0)
    t = lax.rem(lax.broadcasted_iota(jnp.int32, (TOK, width), 1), TOK)
    causal = u <= t
    bias = [jnp.where(level < own_depth, 0.0, NEG).astype(F32) for level in range(UPPER)]
    dk = jnp.zeros(((UPPER + 1) * TOK, HEAD), F32)
    dv = jnp.zeros(((UPPER + 1) * TOK, HEAD), F32)
    for pair in range(GROUP // PAIR):
        cols = [pl.ds((pair * PAIR + m) * HEAD, HEAD) for m in range(PAIR)]
        q = jnp.concatenate([q_ref[:, c] for c in cols], axis=0)
        do = jnp.concatenate([do_ref[:, c] for c in cols], axis=0)
        q_t = q.T
        do_t = do.T
        s = dot(keys, q_t)
        parts = [s[level * TOK:(level + 1) * TOK] + bias[level] for level in range(UPPER)]
        parts.append(jnp.where(causal, s[UPPER * TOK:], NEG))
        s = jnp.concatenate(parts, axis=0)
        top = jnp.max(s, axis=0, keepdims=True)
        w = jnp.exp2((s - top) * (SCALE * LOG2E))
        p = w * (1.0 / jnp.sum(w, axis=0, keepdims=True))
        p_low = p.astype(BF16)
        att_t = dot(values_t, p_low).astype(BF16)
        delta = jnp.sum(do_t.astype(F32) * att_t.astype(F32), axis=0, keepdims=True)
        dp = dot(values, do_t)
        ds = (p * (dp - delta)).astype(BF16)
        dq_t = (dot(keys_t, ds) * SCALE).astype(BF16)
        dv = dv + dot(p_low, do)
        dk = dk + dot(ds, q)
        for m in range(PAIR):
            att_ref[:, cols[m]] = att_t[:, m * TOK:(m + 1) * TOK].T
            dq_ref[:, cols[m]] = dq_t[:, m * TOK:(m + 1) * TOK].T
    dk = dk * SCALE
    for which, grad in enumerate((dk, dv)):
        mine_ref[which, 0] = grad[UPPER * TOK:]
        for level in range(UPPER):
            for part in range(TOK // SLICE):
                first = level * TOK + part * SLICE
                up_ref[which, part, pl.ds(level * SLICE, SLICE), :] = grad[first:first + SLICE].astype(BF16)


def attend(depth, node, queries, out_grad, own, row, col):
    wide = pl.BlockSpec((TOK, GROUP * HEAD), lambda h: (0, h))
    parts = TOK // SLICE
    return pl.pallas_call(
        main_kernel,
        grid=(KV_HEADS,),
        out_shape=(
            jax.ShapeDtypeStruct(queries.shape, BF16),
            jax.ShapeDtypeStruct(queries.shape, BF16),
            jax.ShapeDtypeStruct((2, KV_HEADS * parts, UPPER * SLICE, HEAD), BF16),
            jax.ShapeDtypeStruct((2, KV_HEADS, TOK, HEAD), F32),
        ),
        in_specs=[
            pl.BlockSpec(memory_space=pltpu.SMEM),
            pl.BlockSpec(memory_space=pltpu.SMEM),
            wide,
            wide,
            pl.BlockSpec(memory_space=pl.ANY),
            pl.BlockSpec(memory_space=pl.ANY),
            pl.BlockSpec(memory_space=pl.ANY),
        ],
        out_specs=(
            wide,
            wide,
            pl.BlockSpec((2, parts, UPPER * SLICE, HEAD), lambda h: (0, h, 0, 0)),
            pl.BlockSpec((2, 1, TOK, HEAD), lambda h: (0, h, 0, 0)),
        ),
        scratch_shapes=[
            pltpu.VMEM((UPPER + 1, TOK, 2 * KV_HEADS * HEAD), BF16),
            pltpu.SemaphoreType.DMA((UPPER + 1,)),
        ],
        compiler_params=pltpu.CompilerParams(vmem_limit_bytes=32 * 1024 * 1024),
        name="attend",
    )(depth, node, queries, out_grad, own, row, col)


def owner_kernel(depth_ref, in_ref, out_ref, total):
    total[...] = jnp.zeros_like(total)

    def step(i, last):
        last_one, last_two = last
        owners = (0, last_one, last_two)
        for level in range(UPPER):
            piece = in_ref[i, pl.ds(level * SLICE, SLICE), :].astype(F32)
            total[owners[level]] += piece
        depth = depth_ref[i]
        return (jnp.where(depth == 1, i, last_one), jnp.where(depth == 2, i, last_two))

    lax.fori_loop(0, BLOCKS, step, (jnp.int32(0), jnp.int32(0)))
    out_ref[...] = total[...].astype(BF16)


def sum_by_owner(depth, terms):
    return pl.pallas_call(
        owner_kernel,
        out_shape=jax.ShapeDtypeStruct((BLOCKS, SLICE, HEAD), BF16),
        in_specs=[
            pl.BlockSpec(memory_space=pltpu.SMEM),
            pl.BlockSpec(memory_space=pltpu.VMEM),
        ],
        out_specs=pl.BlockSpec(memory_space=pltpu.VMEM),
        scratch_shapes=[pltpu.VMEM((BLOCKS, SLICE, HEAD), F32)],
        compiler_params=pltpu.CompilerParams(vmem_limit_bytes=16 * 1024 * 1024),
        name="sum_by_owner",
    )(depth, terms)


def finish_kernel(below_ref, mine_ref, dk_ref, dv_ref):
    for which, out_ref in enumerate((dk_ref, dv_ref)):
        for head in range(KV_HEADS):
            grad = mine_ref[which, head] + below_ref[which, head].astype(F32)
            out_ref[:, pl.ds(head * HEAD, HEAD)] = grad.astype(BF16)


def finish(below, mine):
    shape = jax.ShapeDtypeStruct((TOK, KV_HEADS * HEAD), BF16)
    return pl.pallas_call(finish_kernel, out_shape=(shape, shape), name="finish")(below, mine)


def local(queries, key_states, state_values, out_grad, block_depth):
    node = lax.axis_index("node").astype(jnp.int32).reshape(1)
    own = jnp.concatenate([key_states, state_values], axis=1)
    row = lax.all_gather(own, "node", axis_index_groups=Z_GROUPS)
    col = lax.all_gather(pick(block_depth, node, row), "node", axis_index_groups=Y_GROUPS)
    attended, query_grad, up, mine = attend(block_depth, node, queries, out_grad, own, row, col)
    up = up.reshape(BLOCKS, UPPER * SLICE, HEAD)
    terms = lax.all_to_all(up, "node", 0, 0)
    sums = sum_by_owner(block_depth, terms)
    below = lax.all_to_all(sums, "node", 0, 0)
    key_grad, value_grad = finish(below.reshape(2, KV_HEADS, TOK, HEAD), mine)
    return attended, query_grad, key_grad, value_grad


def solution(mesh):
    split = P(("leaf", "node"), None)
    return jax.shard_map(
        local,
        mesh=mesh,
        in_specs=(split, split, split, split, P("leaf")),
        out_specs=(split, split, split, split),
        check_vma=False,
    )
```

```python
import jax
import jax.numpy as jnp
from jax import lax
from jax.experimental import pallas as pl
from jax.experimental.pallas import tpu as pltpu
from jax.sharding import PartitionSpec as P

HEAD = 128
TOK = 128
KV_HEADS = 4
GROUP = 8
BLOCKS = 32
ROWS = 4
COLS = 8
QUAD = 4
HALF = ROWS * QUAD
UPPER = 3
SLICE = 2 * KV_HEADS * TOK // HALF
PARTS = TOK // SLICE
ACROSS = 2 * ROWS + 1
SCALE = HEAD ** -0.5
LOG2E = 1.4426950408889634
NEG = -1e30
F32 = jnp.float32
BF16 = jnp.bfloat16
HALVES = [[y * COLS + h * QUAD + q for y in range(ROWS) for q in range(QUAD)] for h in range(COLS // QUAD)]
SWAP = [(node, node ^ QUAD) for node in range(BLOCKS)]
SMEM = pl.BlockSpec(memory_space=pltpu.SMEM)
VMEM = pl.BlockSpec(memory_space=pltpu.VMEM)


def half_of(node):
    return lax.rem(node, COLS) // QUAD


def member_of(node):
    return (node // COLS) * QUAD + lax.rem(node, QUAD)


def across_of(node, level):
    if level == 0:
        return 2 * ROWS
    return (node // COLS) * 2 + level - 1


def last_in_quad(depth_ref, first, level):
    found = first
    for q in range(QUAD):
        found = jnp.where(depth_ref[first + q] == level, first + q, found)
    return found


def cut_kernel(k_ref, v_ref, out_ref):
    for which, ref in enumerate((k_ref, v_ref)):
        for head in range(KV_HEADS):
            for part in range(PARTS):
                out_ref[(which * KV_HEADS + head) * PARTS + part] = ref[
                    pl.ds(part * SLICE, SLICE), pl.ds(head * HEAD, HEAD)
                ]


def cut(keys, values):
    return pl.pallas_call(
        cut_kernel,
        out_shape=jax.ShapeDtypeStruct((HALF, SLICE, HEAD), BF16),
        in_specs=[VMEM, VMEM],
        out_specs=VMEM,
        name="cut",
    )(keys, values)


def summary_kernel(depth_ref, node_ref, held_ref, out_ref):
    half = half_of(node_ref[0])
    for y in range(ROWS):
        first = y * COLS + half * QUAD
        for level in range(1, UPPER):
            at = last_in_quad(depth_ref, first, level)
            out_ref[across_of(first, level)] = held_ref[member_of(at)]
    out_ref[2 * ROWS] = held_ref[0]


def summary(depth, node, held):
    return pl.pallas_call(
        summary_kernel,
        out_shape=jax.ShapeDtypeStruct((ACROSS, SLICE, HEAD), BF16),
        in_specs=[SMEM, SMEM, VMEM],
        out_specs=VMEM,
        name="summary",
    )(depth, node, held)


def path_kernel(depth_ref, node_ref, held_ref, across_ref, out_ref):
    half = half_of(node_ref[0])

    def step(j, last):
        depth = depth_ref[j]
        last = (jnp.where(depth == 1, j, last[0]), jnp.where(depth == 2, j, last[1]))

        @pl.when(half_of(j) == half)
        def _():
            for level in range(UPPER):
                at = jnp.int32(0) if level == 0 else last[level - 1]
                here = half_of(at) == half
                piece = jnp.where(here, held_ref[member_of(at)], across_ref[across_of(at, level)])
                out_ref[member_of(j), pl.ds(level * SLICE, SLICE), :] = piece

        return last

    lax.fori_loop(0, BLOCKS, step, (jnp.int32(0), jnp.int32(0)))


def paths(depth, node, held, across):
    return pl.pallas_call(
        path_kernel,
        out_shape=jax.ShapeDtypeStruct((HALF, UPPER * SLICE, HEAD), BF16),
        in_specs=[SMEM, SMEM, VMEM, VMEM],
        out_specs=VMEM,
        name="paths",
    )(depth, node, held, across)


def dot(a, b):
    return jnp.dot(a, b, preferred_element_type=F32)


PAIR = 2


def main_kernel(
    depth_ref, node_ref, q_ref, do_ref, k_ref, v_ref, ku_ref, vu_ref,
    att_ref, dq_ref, up_ref, mine_ref,
):
    own_depth = depth_ref[node_ref[0]]

    def path_of(upper_ref, own_ref):
        pieces = [
            upper_ref[0, part, pl.ds(level * SLICE, SLICE), :]
            for level in range(UPPER)
            for part in range(PARTS)
        ]
        return jnp.concatenate(pieces + [own_ref[...]], axis=0)

    keys = path_of(ku_ref, k_ref)
    values = path_of(vu_ref, v_ref)
    keys_t = keys.T
    values_t = values.T
    width = PAIR * TOK
    u = lax.broadcasted_iota(jnp.int32, (TOK, width), 0)
    t = lax.rem(lax.broadcasted_iota(jnp.int32, (TOK, width), 1), TOK)
    causal = u <= t
    bias = [jnp.where(level < own_depth, 0.0, NEG).astype(F32) for level in range(UPPER)]
    dk = jnp.zeros(((UPPER + 1) * TOK, HEAD), F32)
    dv = jnp.zeros(((UPPER + 1) * TOK, HEAD), F32)
    for pair in range(GROUP // PAIR):
        cols = [pl.ds((pair * PAIR + m) * HEAD, HEAD) for m in range(PAIR)]
        q = jnp.concatenate([q_ref[:, c] for c in cols], axis=0)
        do = jnp.concatenate([do_ref[:, c] for c in cols], axis=0)
        q_t = q.T
        do_t = do.T
        s = dot(keys, q_t)
        parts = [s[level * TOK:(level + 1) * TOK] + bias[level] for level in range(UPPER)]
        parts.append(jnp.where(causal, s[UPPER * TOK:], NEG))
        s = jnp.concatenate(parts, axis=0)
        top = jnp.max(s, axis=0, keepdims=True)
        w = jnp.exp2((s - top) * (SCALE * LOG2E))
        p = w * (1.0 / jnp.sum(w, axis=0, keepdims=True))
        p_low = p.astype(BF16)
        att_t = dot(values_t, p_low).astype(BF16)
        delta = jnp.sum(do_t.astype(F32) * att_t.astype(F32), axis=0, keepdims=True)
        dp = dot(values, do_t)
        ds = (p * (dp - delta)).astype(BF16)
        dq_t = (dot(keys_t, ds) * SCALE).astype(BF16)
        dv = dv + dot(p_low, do)
        dk = dk + dot(ds, q)
        for m in range(PAIR):
            att_ref[:, cols[m]] = att_t[:, m * TOK:(m + 1) * TOK].T
            dq_ref[:, cols[m]] = dq_t[:, m * TOK:(m + 1) * TOK].T
    dk = dk * SCALE
    for which, grad in enumerate((dk, dv)):
        mine_ref[which, 0] = grad[UPPER * TOK:]
        for level in range(UPPER):
            for part in range(PARTS):
                first = level * TOK + part * SLICE
                up_ref[which, 0, part, pl.ds(level * SLICE, SLICE), :] = grad[first:first + SLICE].astype(BF16)


def attend(depth, node, queries, out_grad, keys, values, upper):
    upper = upper.reshape(2 * KV_HEADS, PARTS, UPPER * SLICE, HEAD)
    wide = pl.BlockSpec((TOK, GROUP * HEAD), lambda h: (0, h))
    narrow = pl.BlockSpec((TOK, HEAD), lambda h: (0, h))
    upper_block = (1, PARTS, UPPER * SLICE, HEAD)
    return pl.pallas_call(
        main_kernel,
        grid=(KV_HEADS,),
        out_shape=(
            jax.ShapeDtypeStruct(queries.shape, BF16),
            jax.ShapeDtypeStruct(queries.shape, BF16),
            jax.ShapeDtypeStruct((2, KV_HEADS, PARTS, UPPER * SLICE, HEAD), BF16),
            jax.ShapeDtypeStruct((2, KV_HEADS, TOK, HEAD), F32),
        ),
        in_specs=[
            SMEM,
            SMEM,
            wide,
            wide,
            narrow,
            narrow,
            pl.BlockSpec(upper_block, lambda h: (h, 0, 0, 0)),
            pl.BlockSpec(upper_block, lambda h: (KV_HEADS + h, 0, 0, 0)),
        ],
        out_specs=(
            wide,
            wide,
            pl.BlockSpec((2,) + upper_block, lambda h: (0, h, 0, 0, 0)),
            pl.BlockSpec((2, 1, TOK, HEAD), lambda h: (0, h, 0, 0)),
        ),
        compiler_params=pltpu.CompilerParams(vmem_limit_bytes=32 * 1024 * 1024),
        name="attend",
    )(depth, node, queries, out_grad, keys, values, upper, upper)


def owner_kernel(depth_ref, node_ref, terms_ref, own_ref, across_ref, across_sum):
    half = half_of(node_ref[0])
    own_ref[...] = jnp.zeros_like(own_ref)
    across_sum[...] = jnp.zeros_like(across_sum)

    def step(j, last):
        @pl.when(half_of(j) == half)
        def _():
            for level in range(UPPER):
                at = jnp.int32(0) if level == 0 else last[level - 1]
                here = half_of(at) == half
                piece = terms_ref[member_of(j), pl.ds(level * SLICE, SLICE), :].astype(F32)
                own_ref[member_of(at)] += jnp.where(here, piece, 0.0)
                across_sum[across_of(at, level)] += jnp.where(here, 0.0, piece)

        depth = depth_ref[j]
        return (jnp.where(depth == 1, j, last[0]), jnp.where(depth == 2, j, last[1]))

    lax.fori_loop(0, BLOCKS, step, (jnp.int32(0), jnp.int32(0)))
    across_ref[...] = across_sum[...].astype(BF16)


def sum_by_owner(depth, node, terms):
    return pl.pallas_call(
        owner_kernel,
        out_shape=(
            jax.ShapeDtypeStruct((HALF, SLICE, HEAD), F32),
            jax.ShapeDtypeStruct((ACROSS, SLICE, HEAD), BF16),
        ),
        in_specs=[SMEM, SMEM, VMEM],
        out_specs=(VMEM, VMEM),
        scratch_shapes=[pltpu.VMEM((ACROSS, SLICE, HEAD), F32)],
        name="sum_by_owner",
    )(depth, node, terms)


def join_kernel(depth_ref, node_ref, own_ref, across_ref, out_ref, total):
    half = half_of(node_ref[0])
    total[...] = own_ref[...]
    for y in range(ROWS):
        first = y * COLS + half * QUAD
        for level in range(1, UPPER):
            at = last_in_quad(depth_ref, first, level)
            total[member_of(at)] += across_ref[across_of(first, level)].astype(F32)
    total[0] += jnp.where(half == 0, across_ref[2 * ROWS].astype(F32), 0.0)
    out_ref[...] = total[...].astype(BF16)


def join(depth, node, own, across):
    return pl.pallas_call(
        join_kernel,
        out_shape=jax.ShapeDtypeStruct((HALF, SLICE, HEAD), BF16),
        in_specs=[SMEM, SMEM, VMEM, VMEM],
        out_specs=VMEM,
        scratch_shapes=[pltpu.VMEM((HALF, SLICE, HEAD), F32)],
        name="join",
    )(depth, node, own, across)


def finish_kernel(below_ref, mine_ref, dk_ref, dv_ref):
    for which, out_ref in enumerate((dk_ref, dv_ref)):
        for head in range(KV_HEADS):
            for part in range(PARTS):
                rows = pl.ds(part * SLICE, SLICE)
                below = below_ref[(which * KV_HEADS + head) * PARTS + part].astype(F32)
                out_ref[rows, pl.ds(head * HEAD, HEAD)] = (mine_ref[which, head, rows, :] + below).astype(BF16)


def finish(below, mine):
    shape = jax.ShapeDtypeStruct((TOK, KV_HEADS * HEAD), BF16)
    return pl.pallas_call(
        finish_kernel,
        out_shape=(shape, shape),
        in_specs=[VMEM, VMEM],
        out_specs=(VMEM, VMEM),
        name="finish",
    )(below, mine)


def exchange(array):
    return lax.all_to_all(array, "node", 0, 0, axis_index_groups=HALVES)


def local(queries, key_states, state_values, out_grad, block_depth):
    node = lax.axis_index("node").astype(jnp.int32).reshape(1)
    held = exchange(cut(key_states, state_values))
    across = lax.ppermute(summary(block_depth, node, held), "node", SWAP)
    upper = exchange(paths(block_depth, node, held, across))
    attended, query_grad, up, mine = attend(
        block_depth, node, queries, out_grad, key_states, state_values, upper
    )
    terms = exchange(up.reshape(HALF, UPPER * SLICE, HEAD))
    own_sum, across_sum = sum_by_owner(block_depth, node, terms)
    across_sum = lax.ppermute(across_sum, "node", SWAP)
    below = exchange(join(block_depth, node, own_sum, across_sum))
    key_grad, value_grad = finish(below, mine)
    return attended, query_grad, key_grad, value_grad


def solution(mesh):
    split = P(("leaf", "node"), None)
    return jax.shard_map(
        local,
        mesh=mesh,
        in_specs=(split, split, split, split, P("leaf")),
        out_specs=(split, split, split, split),
        check_vma=False,
    )
```

```python
import jax
import jax.numpy as jnp
from jax import lax
from jax.experimental import pallas as pl
from jax.experimental.pallas import tpu as pltpu
from jax.sharding import PartitionSpec as P

HEAD = 128
TOK = 128
KV_HEADS = 4
GROUP = 8
BLOCKS = 32
ROWS = 4
COLS = 8
QUAD = 4
HALF = ROWS * QUAD
UPPER = 3
SLICE = 2 * KV_HEADS * TOK // HALF
PARTS = TOK // SLICE
ACROSS = 2 * ROWS + 1
SCALE = HEAD ** -0.5
LOG2E = 1.4426950408889634
NEG = -1e30
F32 = jnp.float32
BF16 = jnp.bfloat16
HALVES = [[y * COLS + h * QUAD + q for y in range(ROWS) for q in range(QUAD)] for h in range(COLS // QUAD)]
SWAP = [(node, node ^ QUAD) for node in range(BLOCKS)]
SMEM = pl.BlockSpec(memory_space=pltpu.SMEM)
VMEM = pl.BlockSpec(memory_space=pltpu.VMEM)


def small(vmem_mib=4):
    return pltpu.CompilerParams(vmem_limit_bytes=vmem_mib * 1024 * 1024)


def half_of(node):
    return (node >> 2) & 1


def member_of(node):
    return ((node >> 3) << 2) | (node & 3)


def across_of(node, level):
    return ((node >> 3) << 1) + (level - 1)


def slot_of(node, level, half):
    return jnp.where(half_of(node) == half, member_of(node), HALF + across_of(node, level))


def running_last(depth_ref):
    before, upto = [], []
    last = (jnp.int32(0), jnp.int32(0))
    for j in range(BLOCKS):
        before.append(last)
        depth = depth_ref[j]
        last = (jnp.where(depth == 1, j, last[0]), jnp.where(depth == 2, j, last[1]))
        upto.append(last)
    return before, upto


def of_half(table, member, half):
    node = (member // QUAD) * COLS + member % QUAD
    return [jnp.where(half == 0, a, b) for a, b in zip(table[node], table[node + QUAD])]


def last_in_quad(depth_ref, first, level):
    found = first
    for q in range(QUAD):
        found = jnp.where(depth_ref[first + q] == level, first + q, found)
    return found


def cut_kernel(k_ref, v_ref, out_ref):
    for which, ref in enumerate((k_ref, v_ref)):
        for head in range(KV_HEADS):
            for part in range(PARTS):
                out_ref[(which * KV_HEADS + head) * PARTS + part] = ref[
                    pl.ds(part * SLICE, SLICE), pl.ds(head * HEAD, HEAD)
                ]


def cut(keys, values):
    return pl.pallas_call(
        cut_kernel,
        out_shape=jax.ShapeDtypeStruct((HALF, SLICE, HEAD), BF16),
        in_specs=[VMEM, VMEM],
        out_specs=VMEM,
        compiler_params=small(),
        name="cut",
    )(keys, values)


def summary_kernel(depth_ref, node_ref, held_ref, out_ref):
    half = half_of(node_ref[0])
    for y in range(ROWS):
        first = y * COLS + half * QUAD
        for level in range(1, UPPER):
            at = last_in_quad(depth_ref, first, level)
            out_ref[2 * y + level - 1] = held_ref[member_of(at)]
    out_ref[2 * ROWS] = held_ref[0]


def summary(depth, node, held):
    return pl.pallas_call(
        summary_kernel,
        out_shape=jax.ShapeDtypeStruct((ACROSS, SLICE, HEAD), BF16),
        in_specs=[SMEM, SMEM, VMEM],
        out_specs=VMEM,
        compiler_params=small(),
        name="summary",
    )(depth, node, held)


def path_kernel(depth_ref, node_ref, held_ref, across_ref, out_ref, both):
    half = half_of(node_ref[0])
    both[pl.ds(0, HALF)] = held_ref[...]
    both[pl.ds(HALF, ACROSS)] = across_ref[...]
    root = both[jnp.where(half == 0, 0, HALF + 2 * ROWS)]
    _, upto = running_last(depth_ref)
    for member in range(HALF):
        out_ref[member, pl.ds(0, SLICE), :] = root
        for level, at in enumerate(of_half(upto, member, half), start=1):
            out_ref[member, pl.ds(level * SLICE, SLICE), :] = both[slot_of(at, level, half)]


def paths(depth, node, held, across):
    return pl.pallas_call(
        path_kernel,
        out_shape=jax.ShapeDtypeStruct((HALF, UPPER * SLICE, HEAD), BF16),
        in_specs=[SMEM, SMEM, VMEM, VMEM],
        out_specs=VMEM,
        scratch_shapes=[pltpu.VMEM((HALF + ACROSS, SLICE, HEAD), BF16)],
        compiler_params=small(),
        name="paths",
    )(depth, node, held, across)


def dot(a, b):
    return jnp.dot(a, b, preferred_element_type=F32)


def main_kernel(
    depth_ref, node_ref, q_ref, do_ref, k_ref, v_ref, ku_ref, vu_ref,
    att_ref, dq_ref, up_ref, mine_ref,
):
    own_depth = depth_ref[node_ref[0]]

    def path_of(upper_ref, own_ref):
        pieces = [
            upper_ref[0, part, pl.ds(level * SLICE, SLICE), :]
            for level in range(UPPER)
            for part in range(PARTS)
        ]
        return jnp.concatenate(pieces + [own_ref[...]], axis=0)

    keys = path_of(ku_ref, k_ref)
    values = path_of(vu_ref, v_ref)
    width = GROUP * TOK
    u = lax.broadcasted_iota(jnp.int32, (TOK, width), 0)
    t = lax.broadcasted_iota(jnp.int32, (TOK, width), 1) & (TOK - 1)
    heads = [pl.ds(m * HEAD, HEAD) for m in range(GROUP)]
    q = jnp.concatenate([q_ref[:, c] for c in heads], axis=0)
    do = jnp.concatenate([do_ref[:, c] for c in heads], axis=0)
    s = dot(keys, q.T)
    dp = dot(values, do.T)
    parts = []
    for level in range(UPPER):
        bias = jnp.where(level < own_depth, 0.0, NEG).astype(F32)
        parts.append(s[level * TOK:(level + 1) * TOK] + bias)
    parts.append(jnp.where(u <= t, s[UPPER * TOK:], NEG))
    s = jnp.concatenate(parts, axis=0)
    top = jnp.max(s, axis=0, keepdims=True)
    w = jnp.exp2((s - top) * (SCALE * LOG2E))
    p = w * (1.0 / jnp.sum(w, axis=0, keepdims=True))
    p_low = p.astype(BF16)
    delta = jnp.sum(p * dp, axis=0, keepdims=True)
    ds = (p * (dp - delta)).astype(BF16)
    att_t = dot(values.T, p_low).astype(BF16)
    dq_t = (dot(keys.T, ds) * SCALE).astype(BF16)
    dv = dot(p_low, do)
    dk = dot(ds, q) * SCALE
    for m, c in enumerate(heads):
        att_ref[:, c] = att_t[:, m * TOK:(m + 1) * TOK].T
        dq_ref[:, c] = dq_t[:, m * TOK:(m + 1) * TOK].T
    for which, grad in enumerate((dk, dv)):
        mine_ref[which, 0] = grad[UPPER * TOK:]
        for level in range(UPPER):
            for part in range(PARTS):
                first = level * TOK + part * SLICE
                up_ref[which, 0, part, pl.ds(level * SLICE, SLICE), :] = grad[first:first + SLICE].astype(BF16)


def attend(depth, node, queries, out_grad, keys, values, upper):
    upper = upper.reshape(2 * KV_HEADS, PARTS, UPPER * SLICE, HEAD)
    wide = pl.BlockSpec((TOK, GROUP * HEAD), lambda h: (0, h))
    narrow = pl.BlockSpec((TOK, HEAD), lambda h: (0, h))
    upper_block = (1, PARTS, UPPER * SLICE, HEAD)
    return pl.pallas_call(
        main_kernel,
        grid=(KV_HEADS,),
        out_shape=(
            jax.ShapeDtypeStruct(queries.shape, BF16),
            jax.ShapeDtypeStruct(queries.shape, BF16),
            jax.ShapeDtypeStruct((2, KV_HEADS, PARTS, UPPER * SLICE, HEAD), BF16),
            jax.ShapeDtypeStruct((2, KV_HEADS, TOK, HEAD), F32),
        ),
        in_specs=[
            SMEM,
            SMEM,
            wide,
            wide,
            narrow,
            narrow,
            pl.BlockSpec(upper_block, lambda h: (h, 0, 0, 0)),
            pl.BlockSpec(upper_block, lambda h: (KV_HEADS + h, 0, 0, 0)),
        ],
        out_specs=(
            wide,
            wide,
            pl.BlockSpec((2,) + upper_block, lambda h: (0, h, 0, 0, 0)),
            pl.BlockSpec((2, 1, TOK, HEAD), lambda h: (0, h, 0, 0)),
        ),
        compiler_params=small(32),
        name="attend",
    )(depth, node, queries, out_grad, keys, values, upper, upper)


def owner_kernel(depth_ref, node_ref, terms_ref, own_ref, across_ref, both):
    half = half_of(node_ref[0])
    both[...] = jnp.zeros_like(both)
    before, _ = running_last(depth_ref)
    root = jnp.zeros((SLICE, HEAD), F32)
    running = [jnp.zeros((SLICE, HEAD), F32)] * (UPPER - 1)
    previous = [jnp.int32(0)] * (UPPER - 1)
    for member in range(HALF):
        root = root + terms_ref[member, pl.ds(0, SLICE), :].astype(F32)
        for k, at in enumerate(of_half(before, member, half)):
            piece = terms_ref[member, pl.ds((k + 1) * SLICE, SLICE), :].astype(F32)
            running[k] = running[k] * jnp.where(at == previous[k], 1.0, 0.0).astype(F32) + piece
            previous[k] = at
            both[slot_of(at, k + 1, half)] = running[k]
    at_root = jnp.where(half == 0, 0, HALF + 2 * ROWS)
    both[at_root] = both[at_root] + root
    own_ref[...] = both[pl.ds(0, HALF)]
    across_ref[...] = both[pl.ds(HALF, ACROSS)].astype(BF16)


def sum_by_owner(depth, node, terms):
    return pl.pallas_call(
        owner_kernel,
        out_shape=(
            jax.ShapeDtypeStruct((HALF, SLICE, HEAD), F32),
            jax.ShapeDtypeStruct((ACROSS, SLICE, HEAD), BF16),
        ),
        in_specs=[SMEM, SMEM, VMEM],
        out_specs=(VMEM, VMEM),
        scratch_shapes=[pltpu.VMEM((HALF + ACROSS, SLICE, HEAD), F32)],
        compiler_params=small(),
        name="sum_by_owner",
    )(depth, node, terms)


def join_kernel(depth_ref, node_ref, own_ref, across_ref, out_ref):
    half = half_of(node_ref[0])
    for y in range(ROWS):
        first = y * COLS + half * QUAD
        lasts = [last_in_quad(depth_ref, first, level) for level in range(1, UPPER)]
        for q in range(QUAD):
            total = own_ref[y * QUAD + q]
            for k, at in enumerate(lasts):
                chosen = jnp.where(at == first + q, 1.0, 0.0).astype(F32)
                total = total + across_ref[2 * y + k].astype(F32) * chosen
            if y == 0 and q == 0:
                chosen = jnp.where(half == 0, 1.0, 0.0).astype(F32)
                total = total + across_ref[2 * ROWS].astype(F32) * chosen
            out_ref[y * QUAD + q] = total.astype(BF16)


def join(depth, node, own, across):
    return pl.pallas_call(
        join_kernel,
        out_shape=jax.ShapeDtypeStruct((HALF, SLICE, HEAD), BF16),
        in_specs=[SMEM, SMEM, VMEM, VMEM],
        out_specs=VMEM,
        compiler_params=small(),
        name="join",
    )(depth, node, own, across)


def finish_kernel(below_ref, mine_ref, dk_ref, dv_ref):
    for which, out_ref in enumerate((dk_ref, dv_ref)):
        for head in range(KV_HEADS):
            for part in range(PARTS):
                rows = pl.ds(part * SLICE, SLICE)
                below = below_ref[(which * KV_HEADS + head) * PARTS + part].astype(F32)
                out_ref[rows, pl.ds(head * HEAD, HEAD)] = (mine_ref[which, head, rows, :] + below).astype(BF16)


def finish(below, mine):
    shape = jax.ShapeDtypeStruct((TOK, KV_HEADS * HEAD), BF16)
    return pl.pallas_call(
        finish_kernel,
        out_shape=(shape, shape),
        in_specs=[VMEM, VMEM],
        out_specs=(VMEM, VMEM),
        compiler_params=small(),
        name="finish",
    )(below, mine)


def exchange(array):
    return lax.all_to_all(array, "node", 0, 0, axis_index_groups=HALVES)


def local(queries, key_states, state_values, out_grad, block_depth):
    node = lax.axis_index("node").astype(jnp.int32).reshape(1)
    held = exchange(cut(key_states, state_values))
    across = lax.ppermute(summary(block_depth, node, held), "node", SWAP)
    upper = exchange(paths(block_depth, node, held, across))
    attended, query_grad, up, mine = attend(
        block_depth, node, queries, out_grad, key_states, state_values, upper
    )
    terms = exchange(up.reshape(HALF, UPPER * SLICE, HEAD))
    own_sum, across_sum = sum_by_owner(block_depth, node, terms)
    across_sum = lax.ppermute(across_sum, "node", SWAP)
    below = exchange(join(block_depth, node, own_sum, across_sum))
    key_grad, value_grad = finish(below, mine)
    return attended, query_grad, key_grad, value_grad


def solution(mesh):
    split = P(("leaf", "node"), None)
    return jax.shard_map(
        local,
        mesh=mesh,
        in_specs=(split, split, split, split, P("leaf")),
        out_specs=(split, split, split, split),
        check_vma=False,
    )
```

```python
import jax
import jax.numpy as jnp
from jax import lax
from jax.experimental import pallas as pl
from jax.experimental.pallas import tpu as pltpu
from jax.sharding import PartitionSpec as P

HEAD = 128
TOK = 128
KV_HEADS = 4
GROUP = 8
BLOCKS = 32
ROWS = 4
COLS = 8
QUAD = 4
HALF = ROWS * QUAD
UPPER = 3
SLICE = 2 * KV_HEADS * TOK // HALF
PARTS = TOK // SLICE
ACROSS = 2 * ROWS + 1
SCALE = HEAD ** -0.5
LOG2E = 1.4426950408889634
NEG = -1e30
F32 = jnp.float32
BF16 = jnp.bfloat16
ORDER = (
    (2, 2), (1, 1), (0, 0), (0, 1), (2, 1), (1, 0), (1, 2), (0, 2),
    (0, 3), (3, 3), (2, 3), (1, 3), (3, 0), (2, 0), (3, 1), (3, 2),
)
HALVES = [
    [y * COLS + q for y, q in ORDER],
    [y * COLS + COLS - 1 - q for y, q in ORDER],
]
MEMBER = {node: member for half in HALVES for member, node in enumerate(half)}
SWAP = [(node, node - node % COLS + COLS - 1 - node % COLS) for node in range(BLOCKS)]
SMEM = pl.BlockSpec(memory_space=pltpu.SMEM)
VMEM = pl.BlockSpec(memory_space=pltpu.VMEM)


def small(vmem_mib=4):
    return pltpu.CompilerParams(vmem_limit_bytes=vmem_mib * 1024 * 1024)


def half_of(node):
    return (node >> 2) & 1


def slot(node, level, half):
    if node % COLS // QUAD == half:
        return MEMBER[node]
    return HALF + 2 * (node // COLS) + level - 1


def last_slots(depth_ref, half):
    last = [jnp.where(half == 0, slot(0, level, 0), slot(0, level, 1)) for level in range(1, UPPER)]
    before, upto = [], []
    for node in range(BLOCKS):
        before.append(list(last))
        for level in range(1, UPPER):
            here = jnp.where(half == 0, slot(node, level, 0), slot(node, level, 1))
            last[level - 1] = jnp.where(depth_ref[node] == level, here, last[level - 1])
        upto.append(list(last))
    return before, upto


def of_half(table, node, half):
    return [jnp.where(half == 0, a, b) for a, b in zip(table[node], table[node + QUAD])]


def member_at(y, q, half):
    return jnp.where(half == 0, MEMBER[y * COLS + q], MEMBER[y * COLS + QUAD + q])


def last_in_quad(depth_ref, y, level, half):
    found = member_at(y, 0, half)
    for q in range(QUAD):
        depth = jnp.where(half == 0, depth_ref[y * COLS + q], depth_ref[y * COLS + QUAD + q])
        found = jnp.where(depth == level, member_at(y, q, half), found)
    return found


def cut_kernel(k_ref, v_ref, out_ref, sems):
    copies = []
    for which, ref in enumerate((k_ref, v_ref)):
        for head in range(KV_HEADS):
            for part in range(PARTS):
                at = (which * KV_HEADS + head) * PARTS + part
                source = ref.at[pl.ds(part * SLICE, SLICE), pl.ds(head * HEAD, HEAD)]
                copies.append(pltpu.make_async_copy(source, out_ref.at[at], sems.at[at]))
    for copy in copies:
        copy.start()
    for copy in copies:
        copy.wait()


def cut(keys, values):
    return pl.pallas_call(
        cut_kernel,
        out_shape=jax.ShapeDtypeStruct((HALF, SLICE, HEAD), BF16),
        in_specs=[pl.BlockSpec(memory_space=pltpu.HBM)] * 2,
        out_specs=VMEM,
        scratch_shapes=[pltpu.SemaphoreType.DMA((HALF,))],
        compiler_params=small(60),
        name="cut",
    )(keys, values)


def summary_kernel(depth_ref, node_ref, held_ref, out_ref):
    half = half_of(node_ref[0])
    for y in range(ROWS):
        for level in range(1, UPPER):
            out_ref[2 * y + level - 1] = held_ref[last_in_quad(depth_ref, y, level, half)]
    out_ref[2 * ROWS] = held_ref[MEMBER[0]]


def summary(depth, node, held):
    return pl.pallas_call(
        summary_kernel,
        out_shape=jax.ShapeDtypeStruct((ACROSS, SLICE, HEAD), BF16),
        in_specs=[SMEM, SMEM, VMEM],
        out_specs=VMEM,
        compiler_params=small(),
        name="summary",
    )(depth, node, held)


def path_kernel(depth_ref, node_ref, held_ref, across_ref, out_ref, both):
    half = half_of(node_ref[0])
    both[pl.ds(0, HALF)] = held_ref[...]
    both[pl.ds(HALF, ACROSS)] = across_ref[...]
    root = both[jnp.where(half == 0, MEMBER[0], HALF + 2 * ROWS)]
    _, upto = last_slots(depth_ref, half)
    for y in range(ROWS):
        for q in range(QUAD):
            member = member_at(y, q, half)
            out_ref[member, pl.ds(0, SLICE), :] = root
            for level, at in enumerate(of_half(upto, y * COLS + q, half), start=1):
                out_ref[member, pl.ds(level * SLICE, SLICE), :] = both[at]


def paths(depth, node, held, across):
    return pl.pallas_call(
        path_kernel,
        out_shape=jax.ShapeDtypeStruct((HALF, UPPER * SLICE, HEAD), BF16),
        in_specs=[SMEM, SMEM, VMEM, VMEM],
        out_specs=VMEM,
        scratch_shapes=[pltpu.VMEM((HALF + ACROSS, SLICE, HEAD), BF16)],
        compiler_params=small(),
        name="paths",
    )(depth, node, held, across)


def dot(a, b):
    return jnp.dot(a, b, preferred_element_type=F32)


def main_kernel(
    depth_ref, node_ref, q_ref, do_ref, k_ref, v_ref, ku_ref, vu_ref,
    att_ref, dq_ref, up_ref, mine_ref,
):
    own_depth = depth_ref[node_ref[0]]

    def path_of(upper_ref, own_ref):
        pieces = [
            upper_ref[0, part, pl.ds(level * SLICE, SLICE), :]
            for level in range(UPPER)
            for part in range(PARTS)
        ]
        return jnp.concatenate(pieces + [own_ref[...]], axis=0)

    keys = path_of(ku_ref, k_ref)
    values = path_of(vu_ref, v_ref)
    width = GROUP * TOK
    u = lax.broadcasted_iota(jnp.int32, (TOK, width), 0)
    t = lax.broadcasted_iota(jnp.int32, (TOK, width), 1) & (TOK - 1)
    heads = [pl.ds(m * HEAD, HEAD) for m in range(GROUP)]
    q = jnp.concatenate([q_ref[:, c] for c in heads], axis=0)
    do = jnp.concatenate([do_ref[:, c] for c in heads], axis=0)
    s = dot(keys, q.T)
    dp = dot(values, do.T)
    parts = []
    for level in range(UPPER):
        bias = jnp.where(level < own_depth, 0.0, NEG).astype(F32)
        parts.append(s[level * TOK:(level + 1) * TOK] + bias)
    parts.append(jnp.where(u <= t, s[UPPER * TOK:], NEG))
    s = jnp.concatenate(parts, axis=0)
    top = jnp.max(s, axis=0, keepdims=True)
    w = jnp.exp2((s - top) * (SCALE * LOG2E))
    p = w * (1.0 / jnp.sum(w, axis=0, keepdims=True))
    p_low = p.astype(BF16)
    delta = jnp.sum(p * dp, axis=0, keepdims=True)
    ds = (p * (dp - delta)).astype(BF16)
    att_t = dot(values.T, p_low).astype(BF16)
    dq_t = (dot(keys.T, ds) * SCALE).astype(BF16)
    dv = dot(p_low, do)
    dk = dot(ds, q) * SCALE
    for m, c in enumerate(heads):
        att_ref[:, c] = att_t[:, m * TOK:(m + 1) * TOK].T
        dq_ref[:, c] = dq_t[:, m * TOK:(m + 1) * TOK].T
    for which, grad in enumerate((dk, dv)):
        mine_ref[which, 0] = grad[UPPER * TOK:]
        for level in range(UPPER):
            for part in range(PARTS):
                first = level * TOK + part * SLICE
                up_ref[which, 0, part, pl.ds(level * SLICE, SLICE), :] = grad[first:first + SLICE].astype(BF16)


def attend(depth, node, queries, out_grad, keys, values, upper):
    upper = upper.reshape(2 * KV_HEADS, PARTS, UPPER * SLICE, HEAD)
    wide = pl.BlockSpec((TOK, GROUP * HEAD), lambda h: (0, h))
    narrow = pl.BlockSpec((TOK, HEAD), lambda h: (0, h))
    upper_block = (1, PARTS, UPPER * SLICE, HEAD)
    return pl.pallas_call(
        main_kernel,
        grid=(KV_HEADS,),
        out_shape=(
            jax.ShapeDtypeStruct(queries.shape, BF16),
            jax.ShapeDtypeStruct(queries.shape, BF16),
            jax.ShapeDtypeStruct((2, KV_HEADS, PARTS, UPPER * SLICE, HEAD), BF16),
            jax.ShapeDtypeStruct((2, KV_HEADS, TOK, HEAD), F32),
        ),
        in_specs=[
            SMEM,
            SMEM,
            wide,
            wide,
            narrow,
            narrow,
            pl.BlockSpec(upper_block, lambda h: (h, 0, 0, 0)),
            pl.BlockSpec(upper_block, lambda h: (KV_HEADS + h, 0, 0, 0)),
        ],
        out_specs=(
            wide,
            wide,
            pl.BlockSpec((2,) + upper_block, lambda h: (0, h, 0, 0, 0)),
            pl.BlockSpec((2, 1, TOK, HEAD), lambda h: (0, h, 0, 0)),
        ),
        compiler_params=small(32),
        name="attend",
    )(depth, node, queries, out_grad, keys, values, upper, upper)


def owner_kernel(depth_ref, node_ref, terms_ref, own_ref, across_ref, both):
    half = half_of(node_ref[0])
    both[...] = jnp.zeros_like(both)
    before, _ = last_slots(depth_ref, half)
    root = jnp.zeros((SLICE, HEAD), F32)
    running = [jnp.zeros((SLICE, HEAD), F32)] * (UPPER - 1)
    previous = before[0]
    for y in range(ROWS):
        for q in range(QUAD):
            member = member_at(y, q, half)
            root = root + terms_ref[member, pl.ds(0, SLICE), :].astype(F32)
            owners = of_half(before, y * COLS + q, half)
            for k, at in enumerate(owners):
                piece = terms_ref[member, pl.ds((k + 1) * SLICE, SLICE), :].astype(F32)
                running[k] = running[k] * jnp.where(at == previous[k], 1.0, 0.0).astype(F32) + piece
                both[at] = running[k]
            previous = owners
    at_root = jnp.where(half == 0, MEMBER[0], HALF + 2 * ROWS)
    both[at_root] = both[at_root] + root
    own_ref[...] = both[pl.ds(0, HALF)]
    across_ref[...] = both[pl.ds(HALF, ACROSS)].astype(BF16)


def sum_by_owner(depth, node, terms):
    return pl.pallas_call(
        owner_kernel,
        out_shape=(
            jax.ShapeDtypeStruct((HALF, SLICE, HEAD), F32),
            jax.ShapeDtypeStruct((ACROSS, SLICE, HEAD), BF16),
        ),
        in_specs=[SMEM, SMEM, VMEM],
        out_specs=(VMEM, VMEM),
        scratch_shapes=[pltpu.VMEM((HALF + ACROSS, SLICE, HEAD), F32)],
        compiler_params=small(),
        name="sum_by_owner",
    )(depth, node, terms)


def join_kernel(depth_ref, node_ref, own_ref, across_ref, out_ref):
    half = half_of(node_ref[0])
    for y in range(ROWS):
        lasts = [last_in_quad(depth_ref, y, level, half) for level in range(1, UPPER)]
        for q in range(QUAD):
            member = member_at(y, q, half)
            total = own_ref[member]
            for k, at in enumerate(lasts):
                chosen = jnp.where(at == member, 1.0, 0.0).astype(F32)
                total = total + across_ref[2 * y + k].astype(F32) * chosen
            if y == 0 and q == 0:
                chosen = jnp.where(half == 0, 1.0, 0.0).astype(F32)
                total = total + across_ref[2 * ROWS].astype(F32) * chosen
            out_ref[member] = total.astype(BF16)


def join(depth, node, own, across):
    return pl.pallas_call(
        join_kernel,
        out_shape=jax.ShapeDtypeStruct((HALF, SLICE, HEAD), BF16),
        in_specs=[SMEM, SMEM, VMEM, VMEM],
        out_specs=VMEM,
        compiler_params=small(),
        name="join",
    )(depth, node, own, across)


def finish_kernel(below_ref, mine_ref, dk_ref, dv_ref):
    for which, out_ref in enumerate((dk_ref, dv_ref)):
        for head in range(KV_HEADS):
            for part in range(PARTS):
                rows = pl.ds(part * SLICE, SLICE)
                below = below_ref[(which * KV_HEADS + head) * PARTS + part].astype(F32)
                out_ref[rows, pl.ds(head * HEAD, HEAD)] = (mine_ref[which, head, rows, :] + below).astype(BF16)


def finish(below, mine):
    shape = jax.ShapeDtypeStruct((TOK, KV_HEADS * HEAD), BF16)
    return pl.pallas_call(
        finish_kernel,
        out_shape=(shape, shape),
        in_specs=[VMEM, VMEM],
        out_specs=(VMEM, VMEM),
        compiler_params=small(),
        name="finish",
    )(below, mine)


def exchange(array):
    return lax.all_to_all(array, "node", 0, 0, axis_index_groups=HALVES)


def local(queries, key_states, state_values, out_grad, block_depth):
    node = lax.axis_index("node").astype(jnp.int32).reshape(1)
    held = exchange(cut(key_states, state_values))
    across = lax.ppermute(summary(block_depth, node, held), "node", SWAP)
    upper = exchange(paths(block_depth, node, held, across))
    attended, query_grad, up, mine = attend(
        block_depth, node, queries, out_grad, key_states, state_values, upper
    )
    terms = exchange(up.reshape(HALF, UPPER * SLICE, HEAD))
    own_sum, across_sum = sum_by_owner(block_depth, node, terms)
    across_sum = lax.ppermute(across_sum, "node", SWAP)
    below = exchange(join(block_depth, node, own_sum, across_sum))
    key_grad, value_grad = finish(below, mine)
    return attended, query_grad, key_grad, value_grad


def solution(mesh):
    split = P(("leaf", "node"), None)
    return jax.shard_map(
        local,
        mesh=mesh,
        in_specs=(split, split, split, split, P("leaf")),
        out_specs=(split, split, split, split),
        check_vma=False,
    )
```

```python
import jax
import jax.numpy as jnp
from jax import lax
from jax.experimental import pallas as pl
from jax.experimental.pallas import tpu as pltpu
from jax.sharding import PartitionSpec as P

HEAD = 128
TOK = 128
KV_HEADS = 4
GROUP = 8
BLOCKS = 32
ROWS = 4
COLS = 8
QUAD = 4
HALF = ROWS * QUAD
UPPER = 3
SLICE = 2 * KV_HEADS * TOK // HALF
PARTS = TOK // SLICE
ACROSS = 2 * ROWS + 1
ACROSS_BACK = 2 * (ROWS - 1)
SCALE = HEAD ** -0.5
LOG2E = 1.4426950408889634
NEG = -1e30
F32 = jnp.float32
BF16 = jnp.bfloat16
ORDER = (
    (2, 2), (1, 1), (0, 0), (0, 1), (2, 1), (1, 0), (1, 2), (0, 2),
    (0, 3), (3, 3), (2, 3), (1, 3), (3, 0), (2, 0), (3, 1), (3, 2),
)
HALVES = [
    [y * COLS + q for y, q in ORDER],
    [y * COLS + COLS - 1 - q for y, q in ORDER],
]
MEMBER = {node: member for half in HALVES for member, node in enumerate(half)}
TO_SECOND = list(zip(HALVES[0], HALVES[1]))
TO_FIRST = list(zip(HALVES[1], HALVES[0]))
SMEM = pl.BlockSpec(memory_space=pltpu.SMEM)
VMEM = pl.BlockSpec(memory_space=pltpu.VMEM)


def small(vmem_mib=4):
    return pltpu.CompilerParams(vmem_limit_bytes=vmem_mib * 1024 * 1024)


def half_of(node):
    return (node >> 2) & 1


def slot(node, level, half):
    if node % COLS // QUAD == half:
        return MEMBER[node]
    return HALF + 2 * (node // COLS) + level - 1


def last_slots(depth_ref, half):
    last = [jnp.where(half == 0, slot(0, level, 0), slot(0, level, 1)) for level in range(1, UPPER)]
    before, upto = [], []
    for node in range(BLOCKS):
        before.append(list(last))
        for level in range(1, UPPER):
            here = jnp.where(half == 0, slot(node, level, 0), slot(node, level, 1))
            last[level - 1] = jnp.where(depth_ref[node] == level, here, last[level - 1])
        upto.append(list(last))
    return before, upto


def of_half(table, node, half):
    return [jnp.where(half == 0, a, b) for a, b in zip(table[node], table[node + QUAD])]


def member_at(y, q, half):
    return jnp.where(half == 0, MEMBER[y * COLS + q], MEMBER[y * COLS + QUAD + q])


def last_in_quad(depth_ref, y, level, half):
    found = member_at(y, 0, half)
    for q in range(QUAD):
        depth = jnp.where(half == 0, depth_ref[y * COLS + q], depth_ref[y * COLS + QUAD + q])
        found = jnp.where(depth == level, member_at(y, q, half), found)
    return found


def cut_kernel(k_ref, v_ref, out_ref, sems):
    copies = []
    for which, ref in enumerate((k_ref, v_ref)):
        for head in range(KV_HEADS):
            for part in range(PARTS):
                at = (which * KV_HEADS + head) * PARTS + part
                source = ref.at[pl.ds(part * SLICE, SLICE), pl.ds(head * HEAD, HEAD)]
                copies.append(pltpu.make_async_copy(source, out_ref.at[at], sems.at[at]))
    for copy in copies:
        copy.start()
    for copy in copies:
        copy.wait()


def cut(keys, values):
    return pl.pallas_call(
        cut_kernel,
        out_shape=jax.ShapeDtypeStruct((HALF, SLICE, HEAD), BF16),
        in_specs=[pl.BlockSpec(memory_space=pltpu.HBM)] * 2,
        out_specs=VMEM,
        scratch_shapes=[pltpu.SemaphoreType.DMA((HALF,))],
        compiler_params=small(60),
        name="cut",
    )(keys, values)


def summary_kernel(depth_ref, node_ref, held_ref, second_ref, first_ref):
    half = half_of(node_ref[0])
    for y in range(ROWS):
        for level in range(1, UPPER):
            piece = held_ref[last_in_quad(depth_ref, y, level, half)]
            second_ref[2 * y + level - 1] = piece
            if y < ROWS - 1:
                first_ref[2 * y + level - 1] = piece
    second_ref[2 * ROWS] = held_ref[MEMBER[0]]


def summary(depth, node, held):
    return pl.pallas_call(
        summary_kernel,
        out_shape=(
            jax.ShapeDtypeStruct((ACROSS, SLICE, HEAD), BF16),
            jax.ShapeDtypeStruct((ACROSS_BACK, SLICE, HEAD), BF16),
        ),
        in_specs=[SMEM, SMEM, VMEM],
        out_specs=(VMEM, VMEM),
        compiler_params=small(),
        name="summary",
    )(depth, node, held)


def path_kernel(depth_ref, node_ref, held_ref, in_second_ref, in_first_ref, out_ref, both):
    half = half_of(node_ref[0])
    both[pl.ds(0, HALF)] = held_ref[...]

    @pl.when(half == 0)
    def _():
        both[pl.ds(HALF, ACROSS_BACK)] = in_first_ref[...]

    @pl.when(half != 0)
    def _():
        both[pl.ds(HALF, ACROSS)] = in_second_ref[...]

    root = both[jnp.where(half == 0, MEMBER[0], HALF + 2 * ROWS)]
    _, upto = last_slots(depth_ref, half)
    for y in range(ROWS):
        for q in range(QUAD):
            member = member_at(y, q, half)
            out_ref[member, pl.ds(0, SLICE), :] = root
            for level, at in enumerate(of_half(upto, y * COLS + q, half), start=1):
                out_ref[member, pl.ds(level * SLICE, SLICE), :] = both[at]


def paths(depth, node, held, in_second, in_first):
    return pl.pallas_call(
        path_kernel,
        out_shape=jax.ShapeDtypeStruct((HALF, UPPER * SLICE, HEAD), BF16),
        in_specs=[SMEM, SMEM, VMEM, VMEM, VMEM],
        out_specs=VMEM,
        scratch_shapes=[pltpu.VMEM((HALF + ACROSS, SLICE, HEAD), BF16)],
        compiler_params=small(),
        name="paths",
    )(depth, node, held, in_second, in_first)


def dot(a, b):
    return jnp.dot(a, b, preferred_element_type=F32)


def path_of(upper_ref, own_ref, which, head):
    pieces = [
        upper_ref[which * KV_HEADS + head, part, pl.ds(level * SLICE, SLICE), :]
        for level in range(UPPER)
        for part in range(PARTS)
    ]
    return jnp.concatenate(pieces + [own_ref[:, pl.ds(head * HEAD, HEAD)]], axis=0)


def main_kernel(
    depth_ref, node_ref, q_ref, do_ref, k_ref, v_ref, upper_ref,
    att_ref, dq_ref, up_ref, mine_ref,
):
    own_depth = depth_ref[node_ref[0]]
    u = lax.broadcasted_iota(jnp.int32, (TOK, TOK), 0)
    t = lax.broadcasted_iota(jnp.int32, (TOK, TOK), 1)
    biases = [jnp.where(level < own_depth, 0.0, NEG).astype(F32) for level in range(UPPER)]

    def columns(head):
        return [pl.ds((head * GROUP + m) * HEAD, HEAD) for m in range(GROUP)]

    def scores_of(head):
        keys, values = path_of(upper_ref, k_ref, 0, head), path_of(upper_ref, v_ref, 1, head)
        q = jnp.concatenate([q_ref[:, c] for c in columns(head)], axis=0)
        do = jnp.concatenate([do_ref[:, c] for c in columns(head)], axis=0)
        return keys, values, q, do, dot(keys, q.T), dot(values, do.T)

    def probs_of(scores, dprobs):
        p_low, ds = [], []
        for m in range(GROUP):
            s, dp = scores[:, m * TOK:(m + 1) * TOK], dprobs[:, m * TOK:(m + 1) * TOK]
            parts = [s[level * TOK:(level + 1) * TOK] + bias for level, bias in enumerate(biases)]
            parts.append(jnp.where(u <= t, s[UPPER * TOK:], NEG))
            s = jnp.concatenate(parts, axis=0)
            top = jnp.max(s, axis=0, keepdims=True)
            w = jnp.exp2((s - top) * (SCALE * LOG2E))
            p = w * (1.0 / jnp.sum(w, axis=0, keepdims=True))
            delta = jnp.sum(p * dp, axis=0, keepdims=True)
            p_low.append(p.astype(BF16))
            ds.append((p * (dp - delta)).astype(BF16))
        return jnp.concatenate(p_low, axis=1), jnp.concatenate(ds, axis=1)

    later = scores_of(0)
    for head in range(KV_HEADS):
        keys, values, q, do, scores, dprobs = later
        if head + 1 < KV_HEADS:
            later = scores_of(head + 1)
        p_low, ds = probs_of(scores, dprobs)
        att_t = dot(values.T, p_low).astype(BF16)
        dq_t = (dot(keys.T, ds) * SCALE).astype(BF16)
        dv = dot(p_low, do)
        dk = dot(ds, q) * SCALE
        for m, c in enumerate(columns(head)):
            att_ref[:, c] = att_t[:, m * TOK:(m + 1) * TOK].T
            dq_ref[:, c] = dq_t[:, m * TOK:(m + 1) * TOK].T
        for which, grad in enumerate((dk, dv)):
            mine_ref[which, head] = grad[UPPER * TOK:]
            for level in range(UPPER):
                for part in range(PARTS):
                    first = level * TOK + part * SLICE
                    piece = grad[first:first + SLICE].astype(BF16)
                    up_ref[which * KV_HEADS + head, part, pl.ds(level * SLICE, SLICE), :] = piece


def attend(depth, node, queries, out_grad, keys, values, upper):
    upper = upper.reshape(2 * KV_HEADS, PARTS, UPPER * SLICE, HEAD)
    return pl.pallas_call(
        main_kernel,
        out_shape=(
            jax.ShapeDtypeStruct(queries.shape, BF16),
            jax.ShapeDtypeStruct(queries.shape, BF16),
            jax.ShapeDtypeStruct(upper.shape, BF16),
            jax.ShapeDtypeStruct((2, KV_HEADS, TOK, HEAD), F32),
        ),
        in_specs=[SMEM, SMEM] + [VMEM] * 5,
        out_specs=(VMEM,) * 4,
        compiler_params=small(40),
        name="attend",
    )(depth, node, queries, out_grad, keys, values, upper)


def owner_kernel(depth_ref, node_ref, terms_ref, own_ref, first_ref, second_ref, both):
    half = half_of(node_ref[0])
    both[...] = jnp.zeros_like(both)
    before, _ = last_slots(depth_ref, half)
    root = jnp.zeros((SLICE, HEAD), F32)
    running = [jnp.zeros((SLICE, HEAD), F32)] * (UPPER - 1)
    previous = before[0]
    for y in range(ROWS):
        for q in range(QUAD):
            member = member_at(y, q, half)
            root = root + terms_ref[member, pl.ds(0, SLICE), :].astype(F32)
            owners = of_half(before, y * COLS + q, half)
            for k, at in enumerate(owners):
                piece = terms_ref[member, pl.ds((k + 1) * SLICE, SLICE), :].astype(F32)
                running[k] = running[k] * jnp.where(at == previous[k], 1.0, 0.0).astype(F32) + piece
                both[at] = running[k]
            previous = owners
    at_root = jnp.where(half == 0, MEMBER[0], HALF + 2 * ROWS)
    both[at_root] = both[at_root] + root
    own_ref[...] = both[pl.ds(0, HALF)]
    first_ref[...] = both[pl.ds(HALF, ACROSS)].astype(BF16)
    second_ref[...] = both[pl.ds(HALF, ACROSS_BACK)].astype(BF16)


def sum_by_owner(depth, node, terms):
    return pl.pallas_call(
        owner_kernel,
        out_shape=(
            jax.ShapeDtypeStruct((HALF, SLICE, HEAD), F32),
            jax.ShapeDtypeStruct((ACROSS, SLICE, HEAD), BF16),
            jax.ShapeDtypeStruct((ACROSS_BACK, SLICE, HEAD), BF16),
        ),
        in_specs=[SMEM, SMEM, VMEM],
        out_specs=(VMEM, VMEM, VMEM),
        scratch_shapes=[pltpu.VMEM((HALF + ACROSS, SLICE, HEAD), F32)],
        compiler_params=small(),
        name="sum_by_owner",
    )(depth, node, terms)


def join_kernel(depth_ref, node_ref, own_ref, in_first_ref, in_second_ref, out_ref):
    half = half_of(node_ref[0])
    for y in range(ROWS):
        lasts = [last_in_quad(depth_ref, y, level, half) for level in range(1, UPPER)]
        for q in range(QUAD):
            member = member_at(y, q, half)
            total = own_ref[member]
            for k, at in enumerate(lasts):
                chosen = jnp.where(at == member, 1.0, 0.0).astype(F32)
                piece = in_first_ref[2 * y + k].astype(F32)
                if y < ROWS - 1:
                    piece = piece + in_second_ref[2 * y + k].astype(F32)
                total = total + piece * chosen
            if y == 0 and q == 0:
                total = total + in_first_ref[2 * ROWS].astype(F32)
            out_ref[member] = total.astype(BF16)


def join(depth, node, own, in_first, in_second):
    return pl.pallas_call(
        join_kernel,
        out_shape=jax.ShapeDtypeStruct((HALF, SLICE, HEAD), BF16),
        in_specs=[SMEM, SMEM, VMEM, VMEM, VMEM],
        out_specs=VMEM,
        compiler_params=small(),
        name="join",
    )(depth, node, own, in_first, in_second)


def finish_kernel(below_ref, mine_ref, dk_ref, dv_ref):
    for which, out_ref in enumerate((dk_ref, dv_ref)):
        for head in range(KV_HEADS):
            for part in range(PARTS):
                rows = pl.ds(part * SLICE, SLICE)
                below = below_ref[(which * KV_HEADS + head) * PARTS + part].astype(F32)
                out_ref[rows, pl.ds(head * HEAD, HEAD)] = (mine_ref[which, head, rows, :] + below).astype(BF16)


def finish(below, mine):
    shape = jax.ShapeDtypeStruct((TOK, KV_HEADS * HEAD), BF16)
    return pl.pallas_call(
        finish_kernel,
        out_shape=(shape, shape),
        in_specs=[VMEM, VMEM],
        out_specs=(VMEM, VMEM),
        compiler_params=small(),
        name="finish",
    )(below, mine)


def exchange(array):
    return lax.all_to_all(array, "node", 0, 0, axis_index_groups=HALVES)


def local(queries, key_states, state_values, out_grad, block_depth):
    node = lax.axis_index("node").astype(jnp.int32).reshape(1)
    held = exchange(cut(key_states, state_values))
    for_second, for_first = summary(block_depth, node, held)
    in_second = lax.ppermute(for_second, "node", TO_SECOND)
    in_first = lax.ppermute(for_first, "node", TO_FIRST)
    upper = exchange(paths(block_depth, node, held, in_second, in_first))
    attended, query_grad, up, mine = attend(
        block_depth, node, queries, out_grad, key_states, state_values, upper
    )
    terms = exchange(up.reshape(HALF, UPPER * SLICE, HEAD))
    own_sum, for_first, for_second = sum_by_owner(block_depth, node, terms)
    in_first = lax.ppermute(for_first, "node", TO_FIRST)
    in_second = lax.ppermute(for_second, "node", TO_SECOND)
    below = exchange(join(block_depth, node, own_sum, in_first, in_second))
    key_grad, value_grad = finish(below, mine)
    return attended, query_grad, key_grad, value_grad


def solution(mesh):
    split = P(("leaf", "node"), None)
    return jax.shard_map(
        local,
        mesh=mesh,
        in_specs=(split, split, split, split, P("leaf")),
        out_specs=(split, split, split, split),
        check_vma=False,
    )
```

```python
import jax
import jax.numpy as jnp
from jax import lax
from jax.experimental import pallas as pl
from jax.experimental.pallas import tpu as pltpu
from jax.sharding import PartitionSpec as P

HEAD = 128
TOK = 128
KV_HEADS = 4
GROUP = 8
BLOCKS = 32
ROWS = 4
COLS = 8
QUAD = 4
HALF = ROWS * QUAD
UPPER = 3
SLICE = 2 * KV_HEADS * TOK // HALF
PARTS = TOK // SLICE
ACROSS = 2 * ROWS + 1
ACROSS_BACK = 2 * (ROWS - 1)
SCALE = HEAD ** -0.5
LOG2E = 1.4426950408889634
NEG = -1e30
F32 = jnp.float32
BF16 = jnp.bfloat16
PARTNER = (7, 5, 6, 4)
ORDER = (
    (2, 2), (1, 1), (0, 0), (0, 1), (2, 1), (1, 0), (1, 2), (0, 2),
    (0, 3), (3, 3), (2, 3), (1, 3), (3, 0), (2, 0), (3, 1), (3, 2),
)
HALVES = [
    [y * COLS + q for y, q in ORDER],
    [y * COLS + PARTNER[q] for y, q in ORDER],
]
MEMBER = {node: member for half in HALVES for member, node in enumerate(half)}
TO_SECOND = list(zip(HALVES[0], HALVES[1]))
TO_FIRST = list(zip(HALVES[1], HALVES[0]))
SMEM = pl.BlockSpec(memory_space=pltpu.SMEM)
VMEM = pl.BlockSpec(memory_space=pltpu.VMEM)


def small(vmem_mib=4):
    return pltpu.CompilerParams(vmem_limit_bytes=vmem_mib * 1024 * 1024)


def half_of(node):
    return (node >> 2) & 1


def slot(node, level, half):
    if node % COLS // QUAD == half:
        return MEMBER[node]
    return HALF + 2 * (node // COLS) + level - 1


def last_slots(depth_ref, half):
    last = [jnp.where(half == 0, slot(0, level, 0), slot(0, level, 1)) for level in range(1, UPPER)]
    before, upto = [], []
    for node in range(BLOCKS):
        before.append(list(last))
        for level in range(1, UPPER):
            here = jnp.where(half == 0, slot(node, level, 0), slot(node, level, 1))
            last[level - 1] = jnp.where(depth_ref[node] == level, here, last[level - 1])
        upto.append(list(last))
    return before, upto


def of_half(table, node, half):
    return [jnp.where(half == 0, a, b) for a, b in zip(table[node], table[node + QUAD])]


def member_at(y, q, half):
    return jnp.where(half == 0, MEMBER[y * COLS + q], MEMBER[y * COLS + QUAD + q])


def last_in_quad(depth_ref, y, level, half):
    found = member_at(y, 0, half)
    for q in range(QUAD):
        depth = jnp.where(half == 0, depth_ref[y * COLS + q], depth_ref[y * COLS + QUAD + q])
        found = jnp.where(depth == level, member_at(y, q, half), found)
    return found


def cut_kernel(k_ref, v_ref, out_ref, sems):
    copies = []
    for which, ref in enumerate((k_ref, v_ref)):
        for head in range(KV_HEADS):
            for part in range(PARTS):
                at = (which * KV_HEADS + head) * PARTS + part
                source = ref.at[pl.ds(part * SLICE, SLICE), pl.ds(head * HEAD, HEAD)]
                copies.append(pltpu.make_async_copy(source, out_ref.at[at], sems.at[at]))
    for copy in copies:
        copy.start()
    for copy in copies:
        copy.wait()


def cut(keys, values):
    return pl.pallas_call(
        cut_kernel,
        out_shape=jax.ShapeDtypeStruct((HALF, SLICE, HEAD), BF16),
        in_specs=[pl.BlockSpec(memory_space=pltpu.HBM)] * 2,
        out_specs=VMEM,
        scratch_shapes=[pltpu.SemaphoreType.DMA((HALF,))],
        compiler_params=small(60),
        name="cut",
    )(keys, values)


def summary_kernel(depth_ref, node_ref, held_ref, second_ref, first_ref):
    half = half_of(node_ref[0])
    for y in range(ROWS):
        for level in range(1, UPPER):
            piece = held_ref[last_in_quad(depth_ref, y, level, half)]
            second_ref[2 * y + level - 1] = piece
            if y < ROWS - 1:
                first_ref[2 * y + level - 1] = piece
    second_ref[2 * ROWS] = held_ref[MEMBER[0]]


def summary(depth, node, held):
    return pl.pallas_call(
        summary_kernel,
        out_shape=(
            jax.ShapeDtypeStruct((ACROSS, SLICE, HEAD), BF16),
            jax.ShapeDtypeStruct((ACROSS_BACK, SLICE, HEAD), BF16),
        ),
        in_specs=[SMEM, SMEM, VMEM],
        out_specs=(VMEM, VMEM),
        compiler_params=small(),
        name="summary",
    )(depth, node, held)


def path_kernel(depth_ref, node_ref, held_ref, in_second_ref, in_first_ref, out_ref, both):
    half = half_of(node_ref[0])
    both[pl.ds(0, HALF)] = held_ref[...]

    @pl.when(half == 0)
    def _():
        both[pl.ds(HALF, ACROSS_BACK)] = in_first_ref[...]

    @pl.when(half != 0)
    def _():
        both[pl.ds(HALF, ACROSS)] = in_second_ref[...]

    root = both[jnp.where(half == 0, MEMBER[0], HALF + 2 * ROWS)]
    _, upto = last_slots(depth_ref, half)
    for y in range(ROWS):
        for q in range(QUAD):
            member = member_at(y, q, half)
            out_ref[member, pl.ds(0, SLICE), :] = root
            for level, at in enumerate(of_half(upto, y * COLS + q, half), start=1):
                out_ref[member, pl.ds(level * SLICE, SLICE), :] = both[at]


def paths(depth, node, held, in_second, in_first):
    return pl.pallas_call(
        path_kernel,
        out_shape=jax.ShapeDtypeStruct((HALF, UPPER * SLICE, HEAD), BF16),
        in_specs=[SMEM, SMEM, VMEM, VMEM, VMEM],
        out_specs=VMEM,
        scratch_shapes=[pltpu.VMEM((HALF + ACROSS, SLICE, HEAD), BF16)],
        compiler_params=small(),
        name="paths",
    )(depth, node, held, in_second, in_first)


def dot(a, b):
    return jnp.dot(a, b, preferred_element_type=F32)


def path_of(upper_ref, own_ref, which, head):
    pieces = [
        upper_ref[which * KV_HEADS + head, part, pl.ds(level * SLICE, SLICE), :]
        for level in range(UPPER)
        for part in range(PARTS)
    ]
    return jnp.concatenate(pieces + [own_ref[:, pl.ds(head * HEAD, HEAD)]], axis=0)


def main_kernel(
    depth_ref, node_ref, q_ref, do_ref, k_ref, v_ref, upper_ref,
    att_ref, dq_ref, up_ref, mine_ref,
):
    own_depth = depth_ref[node_ref[0]]
    u = lax.broadcasted_iota(jnp.int32, (TOK, TOK), 0)
    t = lax.broadcasted_iota(jnp.int32, (TOK, TOK), 1)
    biases = [jnp.where(level < own_depth, 0.0, NEG).astype(F32) for level in range(UPPER)]

    def columns(head):
        return [pl.ds((head * GROUP + m) * HEAD, HEAD) for m in range(GROUP)]

    def scores_of(head):
        keys, values = path_of(upper_ref, k_ref, 0, head), path_of(upper_ref, v_ref, 1, head)
        q = jnp.concatenate([q_ref[:, c] for c in columns(head)], axis=0)
        do = jnp.concatenate([do_ref[:, c] for c in columns(head)], axis=0)
        return keys, values, q, do, dot(keys, q.T), dot(values, do.T)

    def probs_of(scores, dprobs):
        p_low, ds = [], []
        for m in range(GROUP):
            s, dp = scores[:, m * TOK:(m + 1) * TOK], dprobs[:, m * TOK:(m + 1) * TOK]
            parts = [s[level * TOK:(level + 1) * TOK] + bias for level, bias in enumerate(biases)]
            parts.append(jnp.where(u <= t, s[UPPER * TOK:], NEG))
            s = jnp.concatenate(parts, axis=0)
            top = jnp.max(s, axis=0, keepdims=True)
            w = jnp.exp2((s - top) * (SCALE * LOG2E))
            p = w * (1.0 / jnp.sum(w, axis=0, keepdims=True))
            delta = jnp.sum(p * dp, axis=0, keepdims=True)
            p_low.append(p.astype(BF16))
            ds.append((p * (dp - delta)).astype(BF16))
        return jnp.concatenate(p_low, axis=1), jnp.concatenate(ds, axis=1)

    later = scores_of(0)
    for head in range(KV_HEADS):
        keys, values, q, do, scores, dprobs = later
        if head + 1 < KV_HEADS:
            later = scores_of(head + 1)
        p_low, ds = probs_of(scores, dprobs)
        att_t = dot(values.T, p_low).astype(BF16)
        dq_t = (dot(keys.T, ds) * SCALE).astype(BF16)
        dv = dot(p_low, do)
        dk = dot(ds, q) * SCALE
        for m, c in enumerate(columns(head)):
            att_ref[:, c] = att_t[:, m * TOK:(m + 1) * TOK].T
            dq_ref[:, c] = dq_t[:, m * TOK:(m + 1) * TOK].T
        for which, grad in enumerate((dk, dv)):
            mine_ref[which, head] = grad[UPPER * TOK:]
            for level in range(UPPER):
                for part in range(PARTS):
                    first = level * TOK + part * SLICE
                    piece = grad[first:first + SLICE].astype(BF16)
                    up_ref[which * KV_HEADS + head, part, pl.ds(level * SLICE, SLICE), :] = piece


def attend(depth, node, queries, out_grad, keys, values, upper):
    upper = upper.reshape(2 * KV_HEADS, PARTS, UPPER * SLICE, HEAD)
    return pl.pallas_call(
        main_kernel,
        out_shape=(
            jax.ShapeDtypeStruct(queries.shape, BF16),
            jax.ShapeDtypeStruct(queries.shape, BF16),
            jax.ShapeDtypeStruct(upper.shape, BF16),
            jax.ShapeDtypeStruct((2, KV_HEADS, TOK, HEAD), F32),
        ),
        in_specs=[SMEM, SMEM] + [VMEM] * 5,
        out_specs=(VMEM,) * 4,
        compiler_params=small(40),
        name="attend",
    )(depth, node, queries, out_grad, keys, values, upper)


def owner_kernel(depth_ref, node_ref, terms_ref, own_ref, first_ref, second_ref, both):
    half = half_of(node_ref[0])
    both[...] = jnp.zeros_like(both)
    before, _ = last_slots(depth_ref, half)
    root = jnp.zeros((SLICE, HEAD), F32)
    running = [jnp.zeros((SLICE, HEAD), F32)] * (UPPER - 1)
    previous = before[0]
    for y in range(ROWS):
        for q in range(QUAD):
            member = member_at(y, q, half)
            root = root + terms_ref[member, pl.ds(0, SLICE), :].astype(F32)
            owners = of_half(before, y * COLS + q, half)
            for k, at in enumerate(owners):
                piece = terms_ref[member, pl.ds((k + 1) * SLICE, SLICE), :].astype(F32)
                running[k] = running[k] * jnp.where(at == previous[k], 1.0, 0.0).astype(F32) + piece
                both[at] = running[k]
            previous = owners
    at_root = jnp.where(half == 0, MEMBER[0], HALF + 2 * ROWS)
    both[at_root] = both[at_root] + root
    own_ref[...] = both[pl.ds(0, HALF)]
    first_ref[...] = both[pl.ds(HALF, ACROSS)].astype(BF16)
    second_ref[...] = both[pl.ds(HALF, ACROSS_BACK)].astype(BF16)


def sum_by_owner(depth, node, terms):
    return pl.pallas_call(
        owner_kernel,
        out_shape=(
            jax.ShapeDtypeStruct((HALF, SLICE, HEAD), F32),
            jax.ShapeDtypeStruct((ACROSS, SLICE, HEAD), BF16),
            jax.ShapeDtypeStruct((ACROSS_BACK, SLICE, HEAD), BF16),
        ),
        in_specs=[SMEM, SMEM, VMEM],
        out_specs=(VMEM, VMEM, VMEM),
        scratch_shapes=[pltpu.VMEM((HALF + ACROSS, SLICE, HEAD), F32)],
        compiler_params=small(),
        name="sum_by_owner",
    )(depth, node, terms)


def join_kernel(depth_ref, node_ref, own_ref, in_first_ref, in_second_ref, out_ref):
    half = half_of(node_ref[0])
    for y in range(ROWS):
        lasts = [last_in_quad(depth_ref, y, level, half) for level in range(1, UPPER)]
        for q in range(QUAD):
            member = member_at(y, q, half)
            total = own_ref[member]
            for k, at in enumerate(lasts):
                chosen = jnp.where(at == member, 1.0, 0.0).astype(F32)
                piece = in_first_ref[2 * y + k].astype(F32)
                if y < ROWS - 1:
                    piece = piece + in_second_ref[2 * y + k].astype(F32)
                total = total + piece * chosen
            if y == 0 and q == 0:
                total = total + in_first_ref[2 * ROWS].astype(F32)
            out_ref[member] = total.astype(BF16)


def join(depth, node, own, in_first, in_second):
    return pl.pallas_call(
        join_kernel,
        out_shape=jax.ShapeDtypeStruct((HALF, SLICE, HEAD), BF16),
        in_specs=[SMEM, SMEM, VMEM, VMEM, VMEM],
        out_specs=VMEM,
        compiler_params=small(),
        name="join",
    )(depth, node, own, in_first, in_second)


def finish_kernel(below_ref, mine_ref, dk_ref, dv_ref):
    for which, out_ref in enumerate((dk_ref, dv_ref)):
        for head in range(KV_HEADS):
            for part in range(PARTS):
                rows = pl.ds(part * SLICE, SLICE)
                below = below_ref[(which * KV_HEADS + head) * PARTS + part].astype(F32)
                out_ref[rows, pl.ds(head * HEAD, HEAD)] = (mine_ref[which, head, rows, :] + below).astype(BF16)


def finish(below, mine):
    shape = jax.ShapeDtypeStruct((TOK, KV_HEADS * HEAD), BF16)
    return pl.pallas_call(
        finish_kernel,
        out_shape=(shape, shape),
        in_specs=[VMEM, VMEM],
        out_specs=(VMEM, VMEM),
        compiler_params=small(),
        name="finish",
    )(below, mine)


def exchange(array):
    return lax.all_to_all(array, "node", 0, 0, axis_index_groups=HALVES)


def local(queries, key_states, state_values, out_grad, block_depth):
    node = lax.axis_index("node").astype(jnp.int32).reshape(1)
    held = exchange(cut(key_states, state_values))
    for_second, for_first = summary(block_depth, node, held)
    in_second = lax.ppermute(for_second, "node", TO_SECOND)
    in_first = lax.ppermute(for_first, "node", TO_FIRST)
    upper = exchange(paths(block_depth, node, held, in_second, in_first))
    attended, query_grad, up, mine = attend(
        block_depth, node, queries, out_grad, key_states, state_values, upper
    )
    terms = exchange(up.reshape(HALF, UPPER * SLICE, HEAD))
    own_sum, for_first, for_second = sum_by_owner(block_depth, node, terms)
    in_first = lax.ppermute(for_first, "node", TO_FIRST)
    in_second = lax.ppermute(for_second, "node", TO_SECOND)
    below = exchange(join(block_depth, node, own_sum, in_first, in_second))
    key_grad, value_grad = finish(below, mine)
    return attended, query_grad, key_grad, value_grad


def solution(mesh):
    split = P(("leaf", "node"), None)
    return jax.shard_map(
        local,
        mesh=mesh,
        in_specs=(split, split, split, split, P("leaf")),
        out_specs=(split, split, split, split),
        check_vma=False,
    )
```
